32 devices in a mesh: pairs: 32 (over z, y, x, core).
Axes of the slice: x: 2, y: 2, z: 4, core: 2. Of those that a mesh axis runs over, the one named last changes fastest.
Arguments:
- images: bfloat16 [16384, 1152], P('pairs'), as said below
- texts: bfloat16 [16384, 1152], P('pairs'), as said below
- labels: int32 [16384], P('pairs'), may hold values from 0 to 255
- log_scale: float32 [], replicated, may hold values from 1.8 to 2.8
- bias: float32 [], replicated, may hold values from -12 to -6
Outputs:
- loss: float32 [], replicated
- scale_grad: float32 [], replicated
- bias_grad: float32 [], replicated
- image_grad: bfloat16 [16384, 1152], P('pairs')
- text_grad: bfloat16 [16384, 1152], P('pairs')
The draws below stay inside these ranges and needn't reach their ends.
Inputs may be any that keep to these rules, and one draw needn't show every extreme that they name: `images`: rows of length between 1 and 3. `texts`: rows of length between 1 and 3.
All inputs are finite; a program needn't handle non-finite values.
Results may differ from the reference program's by a relative error of at most 0.001.
The reference program's roundings to bfloat16 on the way (of `weighted`) count: a program that leaves them out, or rounds other values in their place, can miss the bound.
Values may be sent and summed in bfloat16 or wider, within the bound.
A program may use at most 64 MiB of HBM per device.

```python
import jax
import jax.numpy as jnp
from jax import lax

D = 1152
TOK_DEV = 512
TOKENS = 16384
N_PAIRS = 32


def shared_parts(key):
    common_key, pair_key = jax.random.split(key)
    direction = jax.random.normal(common_key, (D,), jnp.float32)
    pairing = jax.random.normal(pair_key, (TOKENS, D), jnp.float32)
    low, high = (0.3, 1.5)
    position = jnp.arange(TOKENS, dtype=jnp.float32) / TOKENS
    strength = low + (high - low) * position
    return (direction, pairing, strength)


def mixed_rows(key, direction, pairing, strength):
    noise = jax.random.normal(key, (TOKENS, D), jnp.float32)
    rows = noise + 0.8 * pairing + strength[:, None] * direction[None, :]
    return rows * D ** (-0.5)


def draw_images(key, part):
    direction, pairing, strength = shared_parts(key)
    key = jax.random.fold_in(key, 11)
    return mixed_rows(key, direction, pairing, strength).astype(jnp.bfloat16)


def draw_texts(key, part):
    direction, pairing, strength = shared_parts(key)
    key = jax.random.fold_in(key, 23)
    return mixed_rows(key, direction, pairing, strength).astype(jnp.bfloat16)


def plant(entries, key, smallest, largest):
    index_at = [jax.random.randint(jax.random.fold_in(key, axis), (), 0, length) for axis, length in enumerate(entries.shape)]
    longest = entries.shape.index(max(entries.shape))
    beside = index_at[:longest] + [(index_at[longest] + 1) % entries.shape[longest]] + index_at[longest + 1:]
    return entries.at[tuple(index_at)].set(smallest).at[tuple(beside)].set(largest)


def setup_inputs(seed: int = 0) -> dict:
    key_list = jax.random.split(jax.random.key(seed), 6)
    return {
        "images": draw_images(jax.random.fold_in(key_list[5], 71), 0),
        "texts": draw_texts(jax.random.fold_in(key_list[5], 71), 0),
        "labels": plant(jax.random.randint(key_list[2], (TOKENS,), 0, 256), jax.random.fold_in(key_list[2], 1), 0, 255).astype(jnp.int32),
        "log_scale": jnp.clip(jax.random.uniform(key_list[3], (), jnp.float32, 1.8, 2.8), 1.8, 2.8),
        "bias": jnp.clip(jax.random.uniform(key_list[4], (), jnp.float32, -12.0, -6.0), -12.0, -6.0),
    }


def normalize(rows):
    return rows * lax.rsqrt(lax.optimization_barrier(jnp.sum(rows * rows, axis=-1, keepdims=True)) + 1e-06)

def tile(x_block, x_tags, y_block, y_tags, scale, bias):
    cosine = lax.dot_general(x_block, y_block, (((1,), (1,)), ((), ())), preferred_element_type=jnp.float32)
    logits = scale * cosine + bias
    sign = jnp.where(x_tags[:, None] == y_tags[None, :], 1.0, -1.0).astype(jnp.float32)
    margin = sign * logits
    summed = jnp.sum(jax.nn.softplus(-margin))
    slope = -sign * jax.nn.sigmoid(-margin)
    weighted = (scale * slope).astype(jnp.bfloat16)
    return (summed, jnp.sum(slope * (logits - bias)), jnp.sum(slope), weighted)

def reference(images, texts, labels, log_scale, bias):
    scale = jnp.exp(log_scale)
    img32 = images.astype(jnp.float32).reshape(N_PAIRS, TOK_DEV, D)
    txt32 = texts.astype(jnp.float32).reshape(N_PAIRS, TOK_DEV, D)
    xnorm = normalize(img32).astype(jnp.bfloat16)
    ynorm = normalize(txt32).astype(jnp.bfloat16)
    tags = labels.reshape(N_PAIRS, TOK_DEV)
    offsets = (0, 1, N_PAIRS // 2)

    def image_side(block):
        grad = jnp.zeros((TOK_DEV, D), jnp.float32)
        sums = [jnp.float32(0.0), jnp.float32(0.0), jnp.float32(0.0)]
        for offset in offsets:
            other = ((block - offset) % N_PAIRS).astype(jnp.int32)
            total, slope_dot, slope_sum, weighted = tile(xnorm[block], tags[block], ynorm[other], tags[other], scale, bias)
            grad = grad + jnp.dot(weighted, ynorm[other], preferred_element_type=jnp.float32)
            sums = [sums[0] + total, sums[1] + slope_dot, sums[2] + slope_sum]
        return (grad, sums[0], sums[1], sums[2])

    def text_side(block):
        grad = jnp.zeros((TOK_DEV, D), jnp.float32)
        for offset in offsets:
            other = ((block + offset) % N_PAIRS).astype(jnp.int32)
            weighted = tile(xnorm[other], tags[other], ynorm[block], tags[block], scale, bias)[3]
            part = lax.dot_general(weighted, xnorm[other], (((0,), (0,)), ((), ())), preferred_element_type=jnp.float32)
            if offset != 0:
                part = lax.optimization_barrier(part.astype(jnp.bfloat16)).astype(jnp.float32)
            grad = grad + part
        return grad
    blocks = jnp.arange(N_PAIRS, dtype=jnp.int32)
    image_dx, totals, slope_dots, slope_sums = lax.map(image_side, blocks)
    text_dy = lax.map(text_side, blocks)
    _, image_pull = jax.vjp(normalize, img32)
    _, text_pull = jax.vjp(normalize, txt32)
    image_grad = image_pull(image_dx)[0].reshape(TOKENS, D).astype(jnp.bfloat16)
    text_grad = text_pull(text_dy)[0].reshape(TOKENS, D).astype(jnp.bfloat16)
    count = jnp.float32(TOKENS)
    return (jnp.sum(totals) / count, jnp.sum(slope_dots) / count, jnp.sum(slope_sums) / count, image_grad, text_grad)
```

```python
import functools

import jax
import jax.numpy as jnp
from jax import lax
from jax.experimental import pallas as pl
from jax.experimental.pallas import tpu as pltpu
from jax.sharding import PartitionSpec as P

MESH = pl.DeviceIdType.MESH
LANES = 128
F32 = jnp.float32
BF16 = jnp.bfloat16


def row_scale(rows):
    return lax.rsqrt(jnp.sum(rows * rows, axis=-1, keepdims=True) + 1e-06)


def kernel(
    n, log_scale_ref, bias_ref, lab_ref, img_hbm, txt_hbm,
    loss_ref, dscale_ref, dbias_ref, gimg_hbm, gtxt_hbm,
    img, txt, xn, yn, xscale, yscale, coltags,
    y_near, x_near, y_far, x_far, lab_prev, lab_next, lab_far,
    dx, dy, dy_near, dy_far, sums, red_out, red_in, gimg, gtxt,
    in_sem, out_sem, yf_s, yf_r, xf_s, xf_r, nr_s, nr_r, lb_s, lb_r, rd_s, rd_r,
):
    tok, width = img.shape
    chunks = tok // LANES
    me = lax.axis_index("pairs")
    after, before = lax.rem(me + 1, n), lax.rem(me + n - 1, n)
    far = lax.rem(me + n // 2, n)
    hops = [1 << s for s in range((n - 1).bit_length())]

    def flip(bit):
        return me + bit - 2 * bit * (lax.rem(me // bit, 2))

    barrier = pltpu.get_barrier_semaphore()
    greeted = [after, before, far] + [flip(b) for b in hops[1:-1]]
    for other in greeted:
        pl.semaphore_signal(barrier, inc=1, device_id=(other,), device_id_type=MESH)
    get_txt = pltpu.make_async_copy(txt_hbm, txt, in_sem.at[0])
    get_img = pltpu.make_async_copy(img_hbm, img, in_sem.at[1])
    get_txt.start()
    get_img.start()
    scale = jnp.exp(jnp.full((8, LANES), log_scale_ref[0, 0], F32))[0:1, :]
    bias = jnp.full((1, LANES), bias_ref[0, 0], F32)

    def remote(src, dst, s, r, to):
        return pltpu.make_async_remote_copy(
            src_ref=src, dst_ref=dst, send_sem=s, recv_sem=r, device_id=(to,), device_id_type=MESH
        )

    def normalized(raw, out, scales):
        @pl.loop(0, chunks)
        def _(j):
            rows = pl.ds(pl.multiple_of(j * LANES, LANES), LANES)
            value = raw[rows, :].astype(F32)
            s = row_scale(value)
            scales[rows, :] = jnp.broadcast_to(s, (LANES, LANES))
            out[rows, :] = (value * s).astype(BF16)

    def part(ref, j):
        return ref.at[pl.ds(j * LANES, LANES), :]

    y_sends = [remote(part(yn, j), part(y_far, j), yf_s.at[j], yf_r.at[j], far) for j in range(chunks)]
    x_sends = [remote(part(xn, j), part(x_far, j), xf_s.at[j], xf_r.at[j], far) for j in range(chunks)]
    y_near_send = remote(yn, y_near, nr_s.at[0], nr_r.at[0], after)
    x_near_send = remote(xn, x_near, nr_s.at[1], nr_r.at[1], before)
    lab_sends = [
        remote(lab_ref, lab_far, lb_s.at[0], lb_r.at[0], far),
        remote(lab_ref, lab_prev, lb_s.at[1], lb_r.at[1], after),
        remote(lab_ref, lab_next, lb_s.at[2], lb_r.at[2], before),
    ]

    get_txt.wait()
    normalized(txt, yn, yscale)
    pl.semaphore_wait(barrier, len(greeted))
    for c in lab_sends:
        c.start()
    for c in y_sends:
        c.start()
    y_near_send.start()
    get_img.wait()
    normalized(img, xn, xscale)
    x_near_send.start()

    for j in range(chunks):
        row = jnp.broadcast_to(lab_ref[j : j + 1, :].astype(F32), (LANES, LANES))
        coltags[j * LANES : (j + 1) * LANES, :] = row.T
    for ref in (dx, dy, dy_near, dy_far, sums):
        ref[...] = jnp.zeros_like(ref)

    def side(local, incoming, labels, total, j, count, with_sums):
        cols = pl.ds(pl.multiple_of(j * count * LANES, count * LANES), count * LANES)

        @pl.loop(0, 2)
        def _(b):
            rows = pl.ds(pl.multiple_of(b * (tok // 2), tok // 2), tok // 2)
            block = incoming[cols, :]
            cosine = lax.dot_general(
                local[rows, :], block, (((1,), (1,)), ((), ())), preferred_element_type=F32
            )
            weights = []
            for c in range(count):
                tags = labels[pl.ds(j * count + c, 1), :].astype(F32)
                logits = scale * cosine[:, c * LANES : (c + 1) * LANES] + bias
                same = coltags[rows, :] == tags
                margin = jnp.where(same, logits, -logits)
                e = jnp.exp(-jnp.abs(logits))
                r = 1.0 / (1.0 + e)
                sig = jnp.where(margin >= 0.0, e * r, r)
                slope = jnp.where(same, -sig, sig)
                weights.append((scale * slope).astype(BF16))
                if with_sums:
                    term = jnp.maximum(-margin, 0.0) + jnp.log1p(e)
                    for i, v in enumerate((term, slope * (logits - bias), slope)):
                        sums[i] += jnp.sum(v.reshape(-1, 8, LANES), axis=0)
            weighted = weights[0] if count == 1 else jnp.concatenate(weights, axis=1)
            total[rows, :] += jnp.dot(weighted, block, preferred_element_type=F32)

    def whole(local, incoming, labels, total, with_sums):
        @pl.loop(0, chunks // 2)
        def _(j):
            side(local, incoming, labels, total, j, 2, with_sums)

    def pulled(raw, scales, grad_of, out, hbm, first_sem):
        copies = []
        for j in range(chunks):
            rows = pl.ds(j * LANES, LANES)
            g = grad_of(rows)
            value = raw[rows, :].astype(F32)
            s = scales[rows, 0:1]
            dots = jnp.sum(g * value, axis=-1, keepdims=True)
            out[rows, :] = (s * g - value * (s * s * s * dots)).astype(BF16)
            copy = pltpu.make_async_copy(out.at[rows, :], hbm.at[rows, :], out_sem.at[first_sem + j])
            copy.start()
            copies.append(copy)
        return copies

    whole(xn, yn, lab_ref, dx, True)
    whole(yn, xn, lab_ref, dy, False)
    for j in range(chunks):
        y_sends[j].wait_send()
        x_sends[j].start()
        y_sends[j].wait_recv()
        if j == 0:
            lab_sends[0].wait_recv()
        side(xn, y_far, lab_far, dx, j, 1, True)
    lab_sends[1].wait_recv()
    y_near_send.wait_recv()
    whole(xn, y_near, lab_prev, dx, True)

    row = lax.broadcasted_iota(jnp.int32, (8, LANES), 0)
    s0, s1, s2 = (jnp.sum(sums[i]) for i in range(3))
    mine = jnp.where(row == 0, s0, jnp.where(row == 1, s1, s2))
    lab_sends[2].wait_recv()
    x_near_send.wait_recv()
    for step, bit in enumerate(hops):
        red_out[step] = mine
        copy = remote(red_out.at[step], red_in.at[step], rd_s.at[step], rd_r.at[step], flip(bit))
        copy.start()
        if step == 0:
            whole(yn, x_near, lab_next, dy_near, False)
        if step == 1:
            out_copies = pulled(img, xscale, lambda rows: dx[rows, :], gimg, gimg_hbm, 0)
        if step == 2:
            dy[...] += dy_near[...].astype(BF16).astype(F32)
        copy.wait()
        mine = mine + red_in[step]
    inverse = 1.0 / (n * tok)
    loss_ref[0, 0] = mine[0, 0] * inverse
    dscale_ref[0, 0] = mine[1, 0] * inverse
    dbias_ref[0, 0] = mine[2, 0] * inverse

    for j in range(chunks):
        x_sends[j].wait_recv()
        side(yn, x_far, lab_far, dy_far, j, 1, False)

    def text_dy(rows):
        return dy[rows, :] + dy_far[rows, :].astype(BF16).astype(F32)

    out_copies += pulled(txt, yscale, text_dy, gtxt, gtxt_hbm, chunks)
    for c in x_sends + lab_sends + [y_near_send, x_near_send]:
        c.wait_send()
    for c in out_copies:
        c.wait()


def per_device(n, images, texts, labels, log_scale, bias):
    tok, width = images.shape
    chunks = tok // LANES
    steps = (n - 1).bit_length()
    smem = pl.BlockSpec(memory_space=pltpu.SMEM)
    vmem = pl.BlockSpec(memory_space=pltpu.VMEM)
    hbm = pl.BlockSpec(memory_space=pltpu.HBM)
    half = lambda: pltpu.VMEM((tok, width), BF16)
    full = lambda: pltpu.VMEM((tok, width), F32)
    tags = lambda: pltpu.VMEM((chunks, LANES), jnp.int32)
    wide = lambda: pltpu.VMEM((tok, LANES), F32)
    dma = lambda k: pltpu.SemaphoreType.DMA((k,))
    scalar = jax.ShapeDtypeStruct((1, 1), F32)
    block = jax.ShapeDtypeStruct((tok, width), BF16)
    loss, dscale, dbias, gimg, gtxt = pl.pallas_call(
        functools.partial(kernel, n),
        out_shape=(scalar, scalar, scalar, block, block),
        in_specs=[smem, smem, vmem, hbm, hbm],
        out_specs=(smem, smem, smem, hbm, hbm),
        scratch_shapes=[
            half(), half(), half(), half(), wide(), wide(), wide(),
            half(), half(), half(), half(), tags(), tags(), tags(),
            full(), full(), full(), full(), pltpu.VMEM((3, 8, LANES), F32),
            pltpu.VMEM((steps, 8, LANES), F32), pltpu.VMEM((steps, 8, LANES), F32), half(), half(),
            dma(2), dma(2 * chunks), dma(chunks), dma(chunks), dma(chunks), dma(chunks),
            dma(2), dma(2), dma(3), dma(3), dma(steps), dma(steps),
        ],
        compiler_params=pltpu.CompilerParams(
            collective_id=0, has_side_effects=True, vmem_limit_bytes=48 * 1024 * 1024
        ),
    )(log_scale.reshape(1, 1), bias.reshape(1, 1), labels.reshape(chunks, LANES), images, texts)
    return (loss.reshape(()), dscale.reshape(()), dbias.reshape(()), gimg, gtxt)


def solution(mesh):
    placed = (P("pairs", None), P("pairs", None), P("pairs"), P(), P())
    return jax.shard_map(
        functools.partial(per_device, mesh.shape["pairs"]),
        mesh=mesh,
        in_specs=placed,
        out_specs=(P(), P(), P(), P("pairs", None), P("pairs", None)),
        check_vma=False,
    )
```

```python
import functools

import jax
import jax.numpy as jnp
from jax import lax
from jax.experimental import pallas as pl
from jax.experimental.pallas import tpu as pltpu
from jax.sharding import PartitionSpec as P

MESH = pl.DeviceIdType.MESH
LANES = 128
F32 = jnp.float32
BF16 = jnp.bfloat16


def row_scale(rows):
    return lax.rsqrt(jnp.sum(rows * rows, axis=-1, keepdims=True) + 1e-06)


def kernel(
    n, log_scale_ref, bias_ref, lab_ref, img_hbm, txt_hbm,
    loss_ref, dscale_ref, dbias_ref, gimg_hbm, gtxt_hbm,
    img, txt, xn, yn, xscale, yscale, coltags,
    y_near, x_near, y_far, x_far, relay, lab_prev, lab_next, lab_far,
    dx, dy, dy_near, dy_far, sums, red_out, red_in, gimg, gtxt,
    in_sem, out_sem, yf_s, yf_r, xf_s, xf_r, nr_s, nr_r, lb_s, lb_r, rd_s, rd_r, rl_s, rl_r,
):
    tok, width = img.shape
    chunks = tok // LANES
    me = lax.axis_index("pairs")
    after, before = lax.rem(me + 1, n), lax.rem(me + n - 1, n)
    far = lax.rem(me + n // 2, n)
    hops = [1 << s for s in range((n - 1).bit_length())]

    def flip(bit):
        return me + bit - 2 * bit * (lax.rem(me // bit, 2))

    relayed = n == 32
    place = lax.rem(me, n // 2)
    across = lax.rem(jnp.where(place < n // 4, me + n - 3, me + 3), n)
    first, last = place == 0, place == n // 2 - 1
    relays_x, relays_y = place == 2, place == n // 2 - 3
    barrier = pltpu.get_barrier_semaphore()
    greeted = [after, before, far] + [flip(b) for b in hops[1:-1]]
    if relayed:
        greeted += [lax.rem(me + 3, n), lax.rem(me + n - 3, n)]
    for other in greeted:
        pl.semaphore_signal(barrier, inc=1, device_id=(other,), device_id_type=MESH)
    get_txt = pltpu.make_async_copy(txt_hbm, txt, in_sem.at[0])
    get_img = pltpu.make_async_copy(img_hbm, img, in_sem.at[1])
    get_txt.start()
    get_img.start()
    scale = jnp.exp(jnp.full((8, LANES), log_scale_ref[0, 0], F32))[0:1, :]
    bias = jnp.full((1, LANES), bias_ref[0, 0], F32)

    def remote(src, dst, s, r, to):
        return pltpu.make_async_remote_copy(
            src_ref=src, dst_ref=dst, send_sem=s, recv_sem=r, device_id=(to,), device_id_type=MESH
        )

    def normalized(raw, out, scales):
        @pl.loop(0, chunks)
        def _(j):
            rows = pl.ds(pl.multiple_of(j * LANES, LANES), LANES)
            value = raw[rows, :].astype(F32)
            s = row_scale(value)
            scales[rows, :] = jnp.broadcast_to(s, (LANES, LANES))
            out[rows, :] = (value * s).astype(BF16)

    def part(ref, j):
        return ref.at[pl.ds(j * LANES, LANES), :]

    y_sends = [remote(part(yn, j), part(y_far, j), yf_s.at[j], yf_r.at[j], far) for j in range(chunks)]
    x_sends = [remote(part(xn, j), part(x_far, j), xf_s.at[j], xf_r.at[j], far) for j in range(chunks)]
    def half(ref, h):
        return ref.at[pl.ds(h * (tok // 2), tok // 2), :]

    y_near_sends = [remote(half(yn, h), half(y_near, h), nr_s.at[h], nr_r.at[h], after) for h in range(2)]
    x_near_sends = [remote(half(xn, h), half(x_near, h), nr_s.at[2 + h], nr_r.at[2 + h], before) for h in range(2)]
    y_detour = remote(half(yn, 1), relay, nr_s.at[1], rl_r.at[0], flip(2))
    x_detour = remote(half(xn, 1), relay, nr_s.at[3], rl_r.at[0], flip(2))
    y_forward = remote(relay, half(y_near, 1), rl_s.at[0], nr_r.at[1], across)
    x_forward = remote(relay, half(x_near, 1), rl_s.at[0], nr_r.at[3], across)

    def send_near(sends, detour, detoured):
        sends[0].start()
        if relayed:
            @pl.when(detoured)
            def _():
                detour.start()

            @pl.when(jnp.logical_not(detoured))
            def _():
                sends[1].start()
        else:
            sends[1].start()

    lab_sends = [
        remote(lab_ref, lab_far, lb_s.at[0], lb_r.at[0], far),
        remote(lab_ref, lab_prev, lb_s.at[1], lb_r.at[1], after),
        remote(lab_ref, lab_next, lb_s.at[2], lb_r.at[2], before),
    ]

    get_txt.wait()
    normalized(txt, yn, yscale)
    pl.semaphore_wait(barrier, len(greeted))
    for c in lab_sends:
        c.start()
    send_near(y_near_sends, y_detour, last)
    for c in y_sends:
        c.start()
    get_img.wait()
    normalized(img, xn, xscale)
    send_near(x_near_sends, x_detour, first)

    for j in range(chunks):
        row = jnp.broadcast_to(lab_ref[j : j + 1, :].astype(F32), (LANES, LANES))
        coltags[j * LANES : (j + 1) * LANES, :] = row.T
    for ref in (dx, dy, dy_near, dy_far, sums):
        ref[...] = jnp.zeros_like(ref)

    def side(local, incoming, labels, total, j, count, with_sums):
        cols = pl.ds(pl.multiple_of(j * count * LANES, count * LANES), count * LANES)

        @pl.loop(0, 2)
        def _(b):
            rows = pl.ds(pl.multiple_of(b * (tok // 2), tok // 2), tok // 2)
            block = incoming[cols, :]
            cosine = lax.dot_general(
                local[rows, :], block, (((1,), (1,)), ((), ())), preferred_element_type=F32
            )
            weights = []
            for c in range(count):
                tags = labels[pl.ds(j * count + c, 1), :].astype(F32)
                logits = scale * cosine[:, c * LANES : (c + 1) * LANES] + bias
                same = coltags[rows, :] == tags
                margin = jnp.where(same, logits, -logits)
                e = jnp.exp(-jnp.abs(logits))
                r = 1.0 / (1.0 + e)
                sig = jnp.where(margin >= 0.0, e * r, r)
                slope = jnp.where(same, -sig, sig)
                weights.append((scale * slope).astype(BF16))
                if with_sums:
                    term = jnp.maximum(-margin, 0.0) + jnp.log1p(e)
                    for i, v in enumerate((term, slope * (logits - bias), slope)):
                        sums[i] += jnp.sum(v.reshape(-1, 8, LANES), axis=0)
            weighted = weights[0] if count == 1 else jnp.concatenate(weights, axis=1)
            total[rows, :] += jnp.dot(weighted, block, preferred_element_type=F32)

    def whole(local, incoming, labels, total, with_sums):
        @pl.loop(0, chunks // 2)
        def _(j):
            side(local, incoming, labels, total, j, 2, with_sums)

    def pulled(raw, scales, grad_of, out, hbm, first_sem):
        copies = []
        for j in range(chunks):
            rows = pl.ds(j * LANES, LANES)
            g = grad_of(rows)
            value = raw[rows, :].astype(F32)
            s = scales[rows, 0:1]
            dots = jnp.sum(g * value, axis=-1, keepdims=True)
            out[rows, :] = (s * g - value * (s * s * s * dots)).astype(BF16)
            copy = pltpu.make_async_copy(out.at[rows, :], hbm.at[rows, :], out_sem.at[first_sem + j])
            copy.start()
            copies.append(copy)
        return copies

    whole(xn, yn, lab_ref, dx, True)
    if relayed:
        @pl.when(relays_y)
        def _():
            y_detour.wait_recv()
            y_forward.start()

        @pl.when(relays_x)
        def _():
            x_detour.wait_recv()
            x_forward.start()

    whole(yn, xn, lab_ref, dy, False)
    for j in range(chunks):
        y_sends[j].wait_send()
        if j > 0:
            x_sends[j - 1].start()
        y_sends[j].wait_recv()
        if j == 0:
            lab_sends[0].wait_recv()
        side(xn, y_far, lab_far, dx, j, 1, True)
    lab_sends[1].wait_recv()
    for c in y_near_sends:
        c.wait_recv()
    whole(xn, y_near, lab_prev, dx, True)

    row = lax.broadcasted_iota(jnp.int32, (8, LANES), 0)
    s0, s1, s2 = (jnp.sum(sums[i]) for i in range(3))
    mine = jnp.where(row == 0, s0, jnp.where(row == 1, s1, s2))
    lab_sends[2].wait_recv()
    for c in x_near_sends:
        c.wait_recv()
    for step, bit in enumerate(hops):
        red_out[step] = mine
        copy = remote(red_out.at[step], red_in.at[step], rd_s.at[step], rd_r.at[step], flip(bit))
        copy.start()
        if step == 0:
            whole(yn, x_near, lab_next, dy_near, False)
        if step == 1:
            out_copies = pulled(img, xscale, lambda rows: dx[rows, :], gimg, gimg_hbm, 0)
        if step == 2:
            dy[...] += dy_near[...].astype(BF16).astype(F32)
        copy.wait()
        mine = mine + red_in[step]
    inverse = 1.0 / (n * tok)
    loss_ref[0, 0] = mine[0, 0] * inverse
    dscale_ref[0, 0] = mine[1, 0] * inverse
    dbias_ref[0, 0] = mine[2, 0] * inverse

    x_sends[0].wait_send()
    x_sends[chunks - 1].start()
    for j in range(chunks):
        x_sends[j].wait_recv()
        side(yn, x_far, lab_far, dy_far, j, 1, False)

    def text_dy(rows):
        return dy[rows, :] + dy_far[rows, :].astype(BF16).astype(F32)

    out_copies += pulled(txt, yscale, text_dy, gtxt, gtxt_hbm, chunks)
    for c in x_sends[1:] + lab_sends + y_near_sends + x_near_sends:
        c.wait_send()
    if relayed:
        @pl.when(relays_y | relays_x)
        def _():
            y_forward.wait_send()

    for c in out_copies:
        c.wait()


def per_device(n, images, texts, labels, log_scale, bias):
    tok, width = images.shape
    chunks = tok // LANES
    steps = (n - 1).bit_length()
    smem = pl.BlockSpec(memory_space=pltpu.SMEM)
    vmem = pl.BlockSpec(memory_space=pltpu.VMEM)
    hbm = pl.BlockSpec(memory_space=pltpu.HBM)
    half = lambda: pltpu.VMEM((tok, width), BF16)
    full = lambda: pltpu.VMEM((tok, width), F32)
    tags = lambda: pltpu.VMEM((chunks, LANES), jnp.int32)
    wide = lambda: pltpu.VMEM((tok, LANES), F32)
    dma = lambda k: pltpu.SemaphoreType.DMA((k,))
    scalar = jax.ShapeDtypeStruct((1, 1), F32)
    block = jax.ShapeDtypeStruct((tok, width), BF16)
    loss, dscale, dbias, gimg, gtxt = pl.pallas_call(
        functools.partial(kernel, n),
        out_shape=(scalar, scalar, scalar, block, block),
        in_specs=[smem, smem, vmem, hbm, hbm],
        out_specs=(smem, smem, smem, hbm, hbm),
        scratch_shapes=[
            half(), half(), half(), half(), wide(), wide(), wide(),
            half(), half(), half(), half(), pltpu.VMEM((tok // 2, width), BF16), tags(), tags(), tags(),
            full(), full(), full(), full(), pltpu.VMEM((3, 8, LANES), F32),
            pltpu.VMEM((steps, 8, LANES), F32), pltpu.VMEM((steps, 8, LANES), F32), half(), half(),
            dma(2), dma(2 * chunks), dma(chunks), dma(chunks), dma(chunks), dma(chunks),
            dma(4), dma(4), dma(3), dma(3), dma(steps), dma(steps), dma(1), dma(1),
        ],
        compiler_params=pltpu.CompilerParams(
            collective_id=0, has_side_effects=True, vmem_limit_bytes=60 * 1024 * 1024
        ),
    )(log_scale.reshape(1, 1), bias.reshape(1, 1), labels.reshape(chunks, LANES), images, texts)
    return (loss.reshape(()), dscale.reshape(()), dbias.reshape(()), gimg, gtxt)


def solution(mesh):
    placed = (P("pairs", None), P("pairs", None), P("pairs"), P(), P())
    return jax.shard_map(
        functools.partial(per_device, mesh.shape["pairs"]),
        mesh=mesh,
        in_specs=placed,
        out_specs=(P(), P(), P(), P("pairs", None), P("pairs", None)),
        check_vma=False,
    )
```

```python
import functools

import jax
import jax.numpy as jnp
from jax import lax
from jax.experimental import pallas as pl
from jax.experimental.pallas import tpu as pltpu
from jax.sharding import PartitionSpec as P

MESH = pl.DeviceIdType.MESH
LANES = 128
F32 = jnp.float32
BF16 = jnp.bfloat16


def row_scale(rows):
    return lax.rsqrt(jnp.sum(rows * rows, axis=-1, keepdims=True) + 1e-06)


def kernel(
    n, log_scale_ref, bias_ref, lab_ref, img_hbm, txt_hbm,
    loss_ref, dscale_ref, dbias_ref, gimg_hbm, gtxt_hbm,
    img, txt, xn, yn, xscale, yscale, coltags,
    y_near, x_near, y_far, x_far, relay, lab_prev, lab_next, lab_far,
    dx, dy, dy_near, dy_far, sums, red_out, red_in, gimg, gtxt,
    in_sem, out_sem, yf_s, yf_r, xf_s, xf_r, nr_s, nr_r, lb_s, lb_r, rd_s, rd_r, rl_s, rl_r,
):
    tok, width = img.shape
    chunks = tok // LANES
    me = lax.axis_index("pairs")
    after, before = lax.rem(me + 1, n), lax.rem(me + n - 1, n)
    far = lax.rem(me + n // 2, n)
    hops = [1 << s for s in range((n - 1).bit_length())]

    def flip(bit):
        return me + bit - 2 * bit * (lax.rem(me // bit, 2))

    relayed = n == 32
    place = lax.rem(me, n // 2)
    across = lax.rem(jnp.where(place < n // 4, me + n - 3, me + 3), n)
    first, last = place == 0, place == n // 2 - 1
    relays_x, relays_y = place == 2, place == n // 2 - 3
    barrier = pltpu.get_barrier_semaphore()
    greeted = [after, before, far] + [flip(b) for b in hops[1:-1]]
    if relayed:
        greeted += [lax.rem(me + 3, n), lax.rem(me + n - 3, n)]
    for other in greeted:
        pl.semaphore_signal(barrier, inc=1, device_id=(other,), device_id_type=MESH)
    get_txt = pltpu.make_async_copy(txt_hbm, txt, in_sem.at[0])
    get_img = pltpu.make_async_copy(img_hbm, img, in_sem.at[1])
    get_txt.start()
    get_img.start()
    scale = jnp.exp(jnp.full((8, LANES), log_scale_ref[0, 0], F32))[0:1, :]
    bias = jnp.full((1, LANES), bias_ref[0, 0], F32)

    def remote(src, dst, s, r, to):
        return pltpu.make_async_remote_copy(
            src_ref=src, dst_ref=dst, send_sem=s, recv_sem=r, device_id=(to,), device_id_type=MESH
        )

    def normalized(raw, out, scales):
        @pl.loop(0, chunks)
        def _(j):
            rows = pl.ds(pl.multiple_of(j * LANES, LANES), LANES)
            value = raw[rows, :].astype(F32)
            s = row_scale(value)
            scales[rows, :] = jnp.broadcast_to(s, (LANES, LANES))
            out[rows, :] = (value * s).astype(BF16)

    def part(ref, j):
        return ref.at[pl.ds(j * LANES, LANES), :]

    y_sends = [remote(part(yn, j), part(y_far, j), yf_s.at[j], yf_r.at[j], far) for j in range(chunks)]
    x_sends = [remote(part(xn, j), part(x_far, j), xf_s.at[j], xf_r.at[j], far) for j in range(chunks)]
    def half(ref, h):
        return ref.at[pl.ds(h * (tok // 2), tok // 2), :]

    y_near_sends = [remote(half(yn, h), half(y_near, h), nr_s.at[h], nr_r.at[h], after) for h in range(2)]
    x_near_sends = [remote(half(xn, h), half(x_near, h), nr_s.at[2 + h], nr_r.at[2 + h], before) for h in range(2)]
    y_detour = remote(half(yn, 1), relay, nr_s.at[1], rl_r.at[0], flip(2))
    x_detour = remote(half(xn, 1), relay, nr_s.at[3], rl_r.at[0], flip(2))
    y_forward = remote(relay, half(y_near, 1), rl_s.at[0], nr_r.at[1], across)
    x_forward = remote(relay, half(x_near, 1), rl_s.at[0], nr_r.at[3], across)

    def send_near(sends, detour, detoured):
        sends[0].start()
        if relayed:
            @pl.when(detoured)
            def _():
                detour.start()

            @pl.when(jnp.logical_not(detoured))
            def _():
                sends[1].start()
        else:
            sends[1].start()

    lab_sends = [
        remote(lab_ref, lab_far, lb_s.at[0], lb_r.at[0], far),
        remote(lab_ref, lab_prev, lb_s.at[1], lb_r.at[1], after),
        remote(lab_ref, lab_next, lb_s.at[2], lb_r.at[2], before),
    ]

    get_txt.wait()
    normalized(txt, yn, yscale)
    pl.semaphore_wait(barrier, len(greeted))
    for c in lab_sends:
        c.start()
    send_near(y_near_sends, y_detour, last)
    get_img.wait()
    normalized(img, xn, xscale)
    send_near(x_near_sends, x_detour, first)
    for c in y_sends:
        c.start()

    for j in range(chunks):
        row = jnp.broadcast_to(lab_ref[j : j + 1, :].astype(F32), (LANES, LANES))
        coltags[j * LANES : (j + 1) * LANES, :] = row.T
    for ref in (dx, dy, dy_near, dy_far, sums):
        ref[...] = jnp.zeros_like(ref)

    def side(local, incoming, labels, total, j, count, with_sums):
        cols = pl.ds(pl.multiple_of(j * count * LANES, count * LANES), count * LANES)

        @pl.loop(0, 2)
        def _(b):
            rows = pl.ds(pl.multiple_of(b * (tok // 2), tok // 2), tok // 2)
            block = incoming[cols, :]
            cosine = lax.dot_general(
                local[rows, :], block, (((1,), (1,)), ((), ())), preferred_element_type=F32
            )
            weights = []
            for c in range(count):
                tags = labels[pl.ds(j * count + c, 1), :].astype(F32)
                logits = scale * cosine[:, c * LANES : (c + 1) * LANES] + bias
                same = coltags[rows, :] == tags
                margin = jnp.where(same, logits, -logits)
                e = jnp.exp(-jnp.abs(logits))
                r = 1.0 / (1.0 + e)
                sig = jnp.where(margin >= 0.0, e * r, r)
                slope = jnp.where(same, -sig, sig)
                weights.append((scale * slope).astype(BF16))
                if with_sums:
                    term = jnp.maximum(-margin, 0.0) + jnp.log1p(e)
                    for i, v in enumerate((term, slope * (logits - bias), slope)):
                        sums[i] += jnp.sum(v.reshape(-1, 8, LANES), axis=0)
            weighted = weights[0] if count == 1 else jnp.concatenate(weights, axis=1)
            total[rows, :] += jnp.dot(weighted, block, preferred_element_type=F32)

    def whole(local, incoming, labels, total, with_sums):
        @pl.loop(0, chunks // 2)
        def _(j):
            side(local, incoming, labels, total, j, 2, with_sums)

    def pulled(raw, scales, grad_of, out, hbm, first_sem):
        copies = []
        for j in range(chunks):
            rows = pl.ds(j * LANES, LANES)
            g = grad_of(rows)
            value = raw[rows, :].astype(F32)
            s = scales[rows, 0:1]
            dots = jnp.sum(g * value, axis=-1, keepdims=True)
            out[rows, :] = (s * g - value * (s * s * s * dots)).astype(BF16)
            copy = pltpu.make_async_copy(out.at[rows, :], hbm.at[rows, :], out_sem.at[first_sem + j])
            copy.start()
            copies.append(copy)
        return copies

    whole(xn, yn, lab_ref, dx, True)
    if relayed:
        @pl.when(relays_y)
        def _():
            y_detour.wait_recv()
            y_forward.start()

        @pl.when(relays_x)
        def _():
            x_detour.wait_recv()
            x_forward.start()

    whole(yn, xn, lab_ref, dy, False)
    for j in range(chunks):
        y_sends[j].wait_send()
        if j > 0:
            x_sends[j - 1].start()
        y_sends[j].wait_recv()
        if j == 0:
            lab_sends[0].wait_recv()
        side(xn, y_far, lab_far, dx, j, 1, True)
    lab_sends[1].wait_recv()
    for c in y_near_sends:
        c.wait_recv()
    whole(xn, y_near, lab_prev, dx, True)

    row = lax.broadcasted_iota(jnp.int32, (8, LANES), 0)
    s0, s1, s2 = (jnp.sum(sums[i]) for i in range(3))
    mine = jnp.where(row == 0, s0, jnp.where(row == 1, s1, s2))
    lab_sends[2].wait_recv()
    for c in x_near_sends:
        c.wait_recv()
    layer = me // (n // 4)
    inner = (layer == 1) | (layer == 2)
    for step, bit in enumerate(hops):
        red_out[step] = mine
        copy = remote(red_out.at[step], red_in.at[step], rd_s.at[step], rd_r.at[step], flip(bit))
        copy.start()
        if step == 0:
            whole(yn, x_near, lab_next, dy_near, False)
        if step == 1:
            out_copies = pulled(img, xscale, lambda rows: dx[rows, :], gimg, gimg_hbm, 0)
        if step == 3:
            @pl.when(inner)
            def _():
                x_sends[0].wait_send()
                x_sends[chunks - 1].start()

        if step == 2:
            dy[...] += dy_near[...].astype(BF16).astype(F32)
        copy.wait()
        mine = mine + red_in[step]
    inverse = 1.0 / (n * tok)
    loss_ref[0, 0] = mine[0, 0] * inverse
    dscale_ref[0, 0] = mine[1, 0] * inverse
    dbias_ref[0, 0] = mine[2, 0] * inverse

    @pl.when(jnp.logical_not(inner))
    def _():
        x_sends[0].wait_send()
        x_sends[chunks - 1].start()

    for j in range(chunks):
        x_sends[j].wait_recv()
        side(yn, x_far, lab_far, dy_far, j, 1, False)

    def text_dy(rows):
        return dy[rows, :] + dy_far[rows, :].astype(BF16).astype(F32)

    out_copies += pulled(txt, yscale, text_dy, gtxt, gtxt_hbm, chunks)
    for c in x_sends[1:] + lab_sends + y_near_sends + x_near_sends:
        c.wait_send()
    if relayed:
        @pl.when(relays_y | relays_x)
        def _():
            y_forward.wait_send()

    for c in out_copies:
        c.wait()


def per_device(n, images, texts, labels, log_scale, bias):
    tok, width = images.shape
    chunks = tok // LANES
    steps = (n - 1).bit_length()
    smem = pl.BlockSpec(memory_space=pltpu.SMEM)
    vmem = pl.BlockSpec(memory_space=pltpu.VMEM)
    hbm = pl.BlockSpec(memory_space=pltpu.HBM)
    half = lambda: pltpu.VMEM((tok, width), BF16)
    full = lambda: pltpu.VMEM((tok, width), F32)
    tags = lambda: pltpu.VMEM((chunks, LANES), jnp.int32)
    wide = lambda: pltpu.VMEM((tok, LANES), F32)
    dma = lambda k: pltpu.SemaphoreType.DMA((k,))
    scalar = jax.ShapeDtypeStruct((1, 1), F32)
    block = jax.ShapeDtypeStruct((tok, width), BF16)
    loss, dscale, dbias, gimg, gtxt = pl.pallas_call(
        functools.partial(kernel, n),
        out_shape=(scalar, scalar, scalar, block, block),
        in_specs=[smem, smem, vmem, hbm, hbm],
        out_specs=(smem, smem, smem, hbm, hbm),
        scratch_shapes=[
            half(), half(), half(), half(), wide(), wide(), wide(),
            half(), half(), half(), half(), pltpu.VMEM((tok // 2, width), BF16), tags(), tags(), tags(),
            full(), full(), full(), full(), pltpu.VMEM((3, 8, LANES), F32),
            pltpu.VMEM((steps, 8, LANES), F32), pltpu.VMEM((steps, 8, LANES), F32), half(), half(),
            dma(2), dma(2 * chunks), dma(chunks), dma(chunks), dma(chunks), dma(chunks),
            dma(4), dma(4), dma(3), dma(3), dma(steps), dma(steps), dma(1), dma(1),
        ],
        compiler_params=pltpu.CompilerParams(
            collective_id=0, has_side_effects=True, vmem_limit_bytes=60 * 1024 * 1024
        ),
    )(log_scale.reshape(1, 1), bias.reshape(1, 1), labels.reshape(chunks, LANES), images, texts)
    return (loss.reshape(()), dscale.reshape(()), dbias.reshape(()), gimg, gtxt)


def solution(mesh):
    placed = (P("pairs", None), P("pairs", None), P("pairs"), P(), P())
    return jax.shard_map(
        functools.partial(per_device, mesh.shape["pairs"]),
        mesh=mesh,
        in_specs=placed,
        out_specs=(P(), P(), P(), P("pairs", None), P("pairs", None)),
        check_vma=False,
    )
```
